32 devices in a mesh: rep: 2 (over y), ep: 4 (over z), tp: 4 (over x, core).
Axes of the slice: x: 2, y: 2, z: 4, core: 2. Of those that a mesh axis runs over, the one named last changes fastest.
Arguments:
- hidden_in: bfloat16 [256, 4096], P(('rep', 'ep')), parts along dimension 0
- queries: bfloat16 [256, 32, 128], P(('rep', 'ep'), 'tp'), parts along dimension 0
- new_keys: bfloat16 [256, 8, 128], P(('rep', 'ep'), 'tp'), parts along dimension 0, may hold values from -6 to 6
- new_values: bfloat16 [256, 8, 128], P(('rep', 'ep'), 'tp'), parts along dimension 0, may hold values from -6 to 6
- key_cache: bfloat16 [256, 8, 256, 128], P(('rep', 'ep'), 'tp'), parts along dimension 0
- value_cache: bfloat16 [256, 8, 256, 128], P(('rep', 'ep'), 'tp'), parts along dimension 0, may hold values from -6 to 6
- lengths: int32 [256], P(('rep', 'ep')), parts along dimension 0, may hold values from 2 to 256
- out_weight: bfloat16 [4096, 4096], P('tp'), may hold values from -0.09375 to 0.09375
- norm_gain: bfloat16 [4096], replicated, may hold values from 0.099609375 to 1.8984375
- router_weight: bfloat16 [4096, 16], replicated, may hold values from -0.1875 to 0.1875
- latent_down: bfloat16 [4096, 1024], P(None, 'tp'), may hold values from -0.09375 to 0.09375
- latent_up: bfloat16 [1024, 4096], P('tp'), may hold values from -0.375 to 0.375
- gate_weight: bfloat16 [16, 1024, 1536], P('ep', None, 'tp'), may hold values from -0.1875 to 0.1875
- up_weight: bfloat16 [16, 1024, 1536], P('ep', None, 'tp'), may hold values from -0.1875 to 0.1875
- down_weight: bfloat16 [16, 1536, 1024], P('ep', 'tp'), may hold values from -0.625 to 0.625
- routes: int32 [256, 16], P('rep'), parts along dimension 0, may hold values from 0 to 15, as said below
- slot_index: int32 [256, 16], P('rep'), parts along dimension 0, may hold values from 0 to 127, as said below
Outputs:
- layer_out: bfloat16 [256, 4096], P(('rep', 'ep', 'tp')), parts along dimension 0
The draws below stay inside these ranges and needn't reach their ends.
There are 2 independent parts, one for each index of `rep`. The reference program is written for one: setup_inputs(seed, part) draws one part's arguments, and reference() takes and returns one part's arrays. A program takes and returns all parts, laid end to end along the dimension named above; an argument that names none is the same for every part. Nothing has to cross between parts.
Inputs may be any that keep to these rules, and one draw needn't show every extreme that they name: `routes`: each row names 16 different experts; one expert, drawn from the seed, is named by every row. slot_index[s,k] counts the rows that name routes[s,k] and come before s in an order of the rows drawn from the seed, so the slots of one expert are distinct; a choice with a slot of 256 or more is dropped.
All inputs are finite; a program needn't handle non-finite values.
Results may differ from the reference program's by a relative error of at most 0.018.
Values may be sent and summed in bfloat16 or wider, within the bound.
A program may use at most 128 MiB of HBM per device.

```python
import math
import jax
import jax.numpy as jnp
from jax import lax

D = 4096
LAT = 1024
FFE = 1536
H = 32
KVH = 8
HD = 128
TOPK = 16
CACHE = 256
TOKENS = 128
EXPERTS = 16
CAPACITY = 256


def route_tables(key):
    key = jax.random.fold_in(key, 11)
    first, second, third, fourth = jax.random.split(key, 4)
    noise = jax.random.randint(first, (TOKENS, EXPERTS), 0, 1 << 19)
    favour = jax.random.randint(second, (EXPERTS,), 0, 1 << 20)
    hottest = jax.random.randint(third, (), 0, EXPERTS)
    ident = jnp.arange(EXPERTS, dtype=jnp.int32)
    score = (noise + favour[None, :]) * EXPERTS + ident[None, :]
    score = jnp.where(ident[None, :] == hottest, jnp.int32(2 ** 30), score)
    unused, chosen = lax.top_k(score, TOPK)
    chosen = chosen.astype(jnp.int32)
    onehot = jnp.sum((chosen[:, :, None] == ident[None, None, :]).astype(jnp.int32), axis=1)
    order = jax.random.permutation(fourth, TOKENS).astype(jnp.int32)
    arranged = onehot[order]
    before_arranged = jnp.cumsum(arranged, axis=0) - arranged
    inverse = jnp.argsort(order, stable=True).astype(jnp.int32)
    before = before_arranged[inverse]
    slots = jnp.take_along_axis(before, chosen, axis=1).astype(jnp.int32)
    return (chosen, slots)


def cache_keys(key):
    key = jax.random.fold_in(key, 12)
    return jax.random.normal(key, (TOKENS, KVH, CACHE, HD), jnp.float32)


def draw_routes(key, part):
    chosen, slots = route_tables(key)
    return chosen


def draw_slot_index(key, part):
    chosen, slots = route_tables(key)
    return slots


def draw_key_cache(key, part):
    keys = cache_keys(key)
    return keys.astype(jnp.bfloat16)


def draw_queries(key, part):
    key = jax.random.fold_in(key, 6)
    values = jax.random.normal(key, (TOKENS, H, HD), jnp.float32)
    return values.astype(jnp.bfloat16)


def draw_lengths(key, part):
    key = jax.random.fold_in(key, 7)
    first, second = jax.random.split(key)
    spans = jax.random.randint(first, (TOKENS,), 2, CACHE + 1)
    longest = jax.random.randint(second, (), 0, TOKENS)
    return jnp.where(jnp.arange(TOKENS) == longest, CACHE, spans).astype(jnp.int32)


def draw_hidden_in(key, part):
    key = jax.random.fold_in(key, 8)
    first = jax.random.fold_in(key, 0)
    values = jax.random.normal(first, (TOKENS, D), jnp.float32)
    return values.astype(jnp.bfloat16)


def block_scale(stream_key, shape, cuts, low, largest):
    loudness = 1.0
    for dim, parts in cuts:
        heights = jax.random.uniform(jax.random.fold_in(jax.random.fold_in(stream_key, 6), dim), (parts,), jnp.float32, low / len(cuts), largest / len(cuts))
        loudness = loudness * jnp.repeat(jnp.exp(heights), shape[dim] // parts).reshape((-1,) + (1,) * (len(shape) - 1 - dim))
    return loudness


def centred(rng, dims, scale, most, cuts=(), kind=jnp.bfloat16):
    values = jax.random.normal(rng, dims, jnp.float32) * scale
    if len(cuts) > 0:
        values = block_scale(rng, dims, cuts, -0.22, 0.18) * values
    return jnp.clip(values, min=-most, max=most).astype(kind)


def setup_inputs(seed: int = 0, part: int = 0) -> dict:
    arg_keys = jax.random.split(jax.random.key(seed), 18)
    part_keys = jax.random.split(jax.random.fold_in(arg_keys[17], part), 18)
    return {
        "hidden_in": draw_hidden_in(jax.random.fold_in(jax.random.fold_in(arg_keys[17], part), 71), part),
        "queries": draw_queries(jax.random.fold_in(jax.random.fold_in(arg_keys[17], part), 71), part),
        "new_keys": centred(part_keys[2], (TOKENS, KVH, HD), 1.0, 6.0, ((0, 4), (1, 4))),
        "new_values": centred(part_keys[3], (TOKENS, KVH, HD), 1.0, 6.0, ((0, 4), (1, 4))),
        "key_cache": draw_key_cache(jax.random.fold_in(jax.random.fold_in(arg_keys[17], part), 71), part),
        "value_cache": centred(part_keys[5], (TOKENS, KVH, CACHE, HD), 1.0, 6.0, ((0, 4), (1, 4))),
        "lengths": draw_lengths(jax.random.fold_in(jax.random.fold_in(arg_keys[17], part), 71), part),
        "out_weight": centred(arg_keys[7], (H * HD, D), (H * HD) ** -0.5, 0.09375, ((0, 4),)),
        "norm_gain": jnp.clip(1.0 + 0.18 * jax.random.normal(arg_keys[8], (D,), jnp.float32), 0.099609375, 1.8984375).astype(jnp.bfloat16),
        "router_weight": centred(arg_keys[9], (D, EXPERTS), (D // 4) ** -0.5, 0.1875),
        "latent_down": centred(arg_keys[10], (D, LAT), D ** -0.5, 0.09375, ((1, 4),)),
        "latent_up": centred(arg_keys[11], (LAT, D), (LAT // 4) ** -0.5, 0.375, ((0, 4),)),
        "gate_weight": centred(arg_keys[12], (EXPERTS, LAT, FFE), LAT ** -0.5, 0.1875, ((0, 4), (2, 4))),
        "up_weight": centred(arg_keys[13], (EXPERTS, LAT, FFE), LAT ** -0.5, 0.1875, ((0, 4), (2, 4))),
        "down_weight": centred(arg_keys[14], (EXPERTS, FFE, LAT), (FFE // 16) ** -0.5, 0.625, ((0, 4), (1, 4))),
        "routes": draw_routes(jax.random.fold_in(jax.random.fold_in(arg_keys[17], part), 71), part),
        "slot_index": draw_slot_index(jax.random.fold_in(jax.random.fold_in(arg_keys[17], part), 71), part),
    }


def attention(queries, new_keys, new_values, key_cache, value_cache, lengths):
    rows, heads, width = queries.shape
    kv_heads = new_keys.shape[1]
    grouped = queries.reshape(rows, kv_heads, heads // kv_heads, width).astype(jnp.float32)
    scale = 1.0 / math.sqrt(width)
    cached = jnp.einsum('skgd,skpd->skgp', grouped, key_cache.astype(jnp.float32)) * scale
    own = jnp.einsum('skgd,skd->skg', grouped, new_keys.astype(jnp.float32)) * scale
    valid = jnp.arange(key_cache.shape[2], dtype=jnp.int32)[None, :] < lengths[:, None]
    cached = jnp.where(valid[:, None, None, :], cached, -jnp.inf)
    top = jnp.maximum(lax.optimization_barrier(jnp.max(cached, axis=-1)), own)
    expos = jnp.exp(cached - top[..., None])
    own_expo = jnp.exp(own - top)
    total = lax.optimization_barrier(jnp.sum(expos, axis=-1)) + own_expo
    probs = (expos / total[..., None]).astype(jnp.bfloat16)
    own_probs = (own_expo / total).astype(jnp.bfloat16)
    mixed = jnp.einsum('skgp,skpd->skgd', probs.astype(jnp.float32), value_cache.astype(jnp.float32))
    mixed = mixed + own_probs.astype(jnp.float32)[..., None] * new_values.astype(jnp.float32)[:, :, None, :]
    return mixed.reshape(rows, heads * width).astype(jnp.bfloat16)

def rms_norm(values, norm_gain):
    mean_sq = lax.optimization_barrier(jnp.mean(values * values, axis=-1, keepdims=True))
    return (values * lax.rsqrt(mean_sq + 1e-05) * norm_gain.astype(jnp.float32)).astype(jnp.bfloat16)

def reference(hidden_in, queries, new_keys, new_values, key_cache, value_cache, lengths, out_weight, norm_gain, router_weight, latent_down, latent_up, gate_weight, up_weight, down_weight, routes, slot_index):
    attended = attention(queries, new_keys, new_values, key_cache, value_cache, lengths)
    residual = hidden_in.astype(jnp.float32) + jnp.dot(attended, out_weight, preferred_element_type=jnp.float32)
    normed = rms_norm(residual, norm_gain)
    latent = jnp.dot(normed, latent_down, preferred_element_type=jnp.float32).astype(jnp.bfloat16)
    logits = jnp.dot(normed, router_weight, preferred_element_type=jnp.float32)
    gates = jax.nn.sigmoid(logits)
    experts_all = router_weight.shape[1]
    ident = jnp.arange(experts_all, dtype=jnp.int32)
    chosen = routes[:, :, None] == ident[None, None, :]
    picked = lax.optimization_barrier(jnp.sum(chosen, axis=1)).astype(jnp.float32)
    kept = lax.optimization_barrier(jnp.sum(chosen & (slot_index[:, :, None] < CAPACITY), axis=1)).astype(jnp.float32)
    weights = kept * gates / lax.optimization_barrier(jnp.sum(picked * gates, axis=-1, keepdims=True))
    slot_of = lax.optimization_barrier(jnp.sum(jnp.where(chosen, slot_index[:, :, None], 0), axis=1))
    slot_of = jnp.where(jnp.any(chosen, axis=1), slot_of, CAPACITY).astype(jnp.int32)

    def one_expert(inputs):
        slot_col, w_gate, w_up, w_down = inputs
        placing = (jnp.arange(CAPACITY, dtype=jnp.int32)[:, None] == slot_col[None, :]).astype(jnp.bfloat16)
        filled = jnp.dot(placing, latent, preferred_element_type=jnp.float32).astype(jnp.bfloat16)
        gate = jnp.dot(filled, w_gate, preferred_element_type=jnp.float32)
        upper = jnp.dot(filled, w_up, preferred_element_type=jnp.float32)
        active = (jax.nn.silu(gate) * upper).astype(jnp.bfloat16)
        outputs = jnp.dot(active, w_down, preferred_element_type=jnp.float32).astype(jnp.bfloat16)
        return jnp.dot(placing.T, outputs, preferred_element_type=jnp.float32)
    per_expert = lax.map(one_expert, (slot_of.T, gate_weight, up_weight, down_weight))
    combined = jnp.einsum('gx,xgl->gl', weights, per_expert).astype(jnp.bfloat16)
    lifted = jnp.dot(combined, latent_up, preferred_element_type=jnp.float32)
    return (residual + lifted).astype(jnp.bfloat16)
```

```python
import functools
import math

import jax
import jax.numpy as jnp
from jax import lax
from jax.experimental import pallas as pl
from jax.experimental.pallas import tpu as pltpu
from jax.sharding import PartitionSpec as P

MESH = pl.DeviceIdType.MESH
F32 = jnp.float32
BF16 = jnp.bfloat16


def dot(a, b):
    return jnp.dot(a, b, preferred_element_type=F32)


def dot_nt(a, b):
    return lax.dot_general(a, b, (((1,), (1,)), ((), ())), preferred_element_type=F32)


def layer_kernel(
    dims,
    hidden_ref,
    q_ref,
    nk_ref,
    nv_ref,
    k_hbm,
    v_hbm,
    len_ref,
    wo_hbm,
    gain_ref,
    router_hbm,
    wd_hbm,
    wu_hbm,
    wg_hbm,
    wp_hbm,
    wn_hbm,
    routes_ref,
    slots_ref,
    out_ref,
    kbuf,
    vbuf,
    wo,
    router,
    wd,
    wu,
    wg,
    wp,
    wn,
    hid,
    att,
    p_own,
    p_send,
    p_recv,
    res,
    n_all,
    lat_all,
    w_all,
    act,
    c_own,
    c_send,
    c_recv,
    d_send,
    d_recv,
    l_own,
    l_send,
    l_recv,
    kv_sem,
    w_sem,
    s1,
    r1,
    s2,
    r2,
    s3,
    r3,
    s3w,
    r3w,
    s4,
    r4,
    s5,
    r5,
    s6,
    r6,
    s7,
    r7,
):
    (T, E, R, r, D, NC, L, X, XA, F, N, TOPK, slots_all) = dims
    me = lax.axis_index("tp")
    ep = lax.axis_index("ep")
    CW = D // NC
    Hl, HD = q_ref.shape[1], q_ref.shape[2]
    G = nk_ref.shape[1]
    grp = Hl // G
    CACHE = k_hbm.shape[2]
    AC = 8
    NA = R // AC

    def tp_peer(k):
        return lax.rem(me + k, T)

    def ep_peer(i):
        return lax.rem(ep + i, E)

    def kv_copy(c, which):
        src, dst = ((k_hbm, kbuf), (v_hbm, vbuf))[which]
        rows = pl.ds(c * AC, AC)
        return pltpu.make_async_copy(src.at[rows], dst.at[rows], kv_sem.at[which, c])

    for c in range(NA):
        kv_copy(c, 0).start()
        kv_copy(c, 1).start()
    hid_copy = pltpu.make_async_copy(hidden_ref.at[me], hid, w_sem.at[0])
    loads = [
        pltpu.make_async_copy(src, dst, w_sem.at[i + 1])
        for i, (src, dst) in enumerate(
            (
                (wo_hbm, wo),
                (wd_hbm, wd),
                (router_hbm, router),
                (wg_hbm, wg),
                (wp_hbm, wp),
                (wn_hbm, wn),
                (wu_hbm, wu),
            )
        )
    ]
    loads[0].start()
    hid_copy.start()

    barrier = pltpu.get_barrier_semaphore()
    for k in range(1, T):
        pl.semaphore_signal(barrier, inc=1, device_id={"tp": tp_peer(k)}, device_id_type=MESH)
    for i in range(1, E):
        pl.semaphore_signal(barrier, inc=1, device_id={"ep": ep_peer(i)}, device_id_type=MESH)

    for load in loads[1:]:
        load.start()

    scale = 1.0 / math.sqrt(HD)

    def by_group(pieces, width):
        row = lax.broadcasted_iota(jnp.int32, (Hl, width), 0)
        value = jnp.broadcast_to(pieces[0], (Hl, width))
        for g in range(1, G):
            value = jnp.where(row >= g * grp, jnp.broadcast_to(pieces[g], (Hl, width)), value)
        return value

    def attend(c, carry):
        kv_copy(c, 0).wait()
        scores, owns = [], []
        column = lax.broadcasted_iota(jnp.int32, (Hl, CACHE), 1)
        for i in range(AC):
            s = c * AC + i
            qs = q_ref[s]
            sc = by_group([dot_nt(qs, kbuf[s, g]) for g in range(G)], CACHE) * scale
            scores.append(jnp.where(column < len_ref[s], sc, -jnp.inf))
            nks = nk_ref[s].astype(F32)
            nkx = by_group([nks[g : g + 1] for g in range(G)], HD)
            owns.append(jnp.sum(qs.astype(F32) * nkx, axis=-1, keepdims=True) * scale)
        kv_copy(c, 1).wait()
        probs, own_probs = [], []
        for i in range(AC):
            top = jnp.maximum(jnp.max(scores[i], axis=-1, keepdims=True), owns[i])
            expo = jnp.exp(scores[i] - top)
            own_expo = jnp.exp(owns[i] - top)
            total = jnp.sum(expo, axis=-1, keepdims=True) + own_expo
            probs.append((expo / total).astype(BF16))
            own_probs.append((own_expo / total).astype(BF16).astype(F32))
        for i in range(AC):
            s = c * AC + i
            mixed = by_group([dot(probs[i], vbuf[s, g]) for g in range(G)], HD)
            nvs = nv_ref[s].astype(F32)
            nvx = by_group([nvs[g : g + 1] for g in range(G)], HD)
            att[s] = mixed + own_probs[i] * nvx
        return carry

    lax.fori_loop(0, NA, attend, 0)
    attended = jnp.concatenate([att[:, h, :] for h in range(Hl)], axis=1).astype(BF16)

    pl.semaphore_wait(barrier, T - 1 + E - 1)

    def p_copy(c, k):
        peer = tp_peer(k)
        return pltpu.make_async_remote_copy(
            src_ref=p_send.at[c, peer],
            dst_ref=p_recv.at[c, k - 1],
            send_sem=s1.at[c, k - 1],
            recv_sem=r1.at[c, k - 1],
            device_id={"tp": peer},
            device_id_type=MESH,
        )

    loads[0].wait()

    def project(c, carry):
        cols = pl.ds(pl.multiple_of(c * CW, CW), CW)
        part = dot(attended, wo[:, cols]).reshape(T, r, CW)
        p_own[c] = part
        p_send[c] = part.astype(BF16)
        for k in range(1, T):
            p_copy(c, k).start()
        return carry

    lax.fori_loop(0, NC, project, 0)

    hid_copy.wait()
    sumsq = jnp.zeros((r, 1), F32)
    for c in range(NC):
        value = hid[:, c * CW : (c + 1) * CW].astype(F32) + p_own[c, me]
        for k in range(1, T):
            p_copy(c, k).wait_recv()
            value = value + p_recv[c, k - 1].astype(F32)
        res[c] = value
        sumsq = sumsq + jnp.sum(value * value, axis=-1, keepdims=True)
    inv = lax.rsqrt(sumsq * (1.0 / D) + 1e-05)
    for c in range(NC):
        gain = gain_ref[:, c * CW : (c + 1) * CW].astype(F32)
        n_all[me, c] = (res[c] * inv * gain).astype(BF16)

    def n_copy(k):
        peer = tp_peer(k)
        return pltpu.make_async_remote_copy(
            src_ref=n_all.at[me],
            dst_ref=n_all.at[me],
            send_sem=s2.at[k - 1],
            recv_sem=r2.at[k - 1],
            device_id={"tp": peer},
            device_id_type=MESH,
        )

    for k in range(1, T):
        n_copy(k).start()

    blk = pl.ds(pl.multiple_of(ep * R, R), R)
    ident = lax.broadcasted_iota(jnp.int32, (R, XA), 1)
    routes = routes_ref[blk, :]
    slots = slots_ref[blk, :]
    picked = jnp.zeros((R, XA), F32)
    kept = jnp.zeros((R, XA), F32)
    for k in range(TOPK):
        hit = jnp.where(routes[:, k : k + 1] == ident, 1.0, 0.0)
        picked = picked + hit
        kept = kept + jnp.where(slots[:, k : k + 1] < slots_all, hit, 0.0)

    loads[1].wait()
    loads[2].wait()
    for k in range(1, T):
        n_copy(k).wait_recv()
    pieces = [n_all[:, c].astype(F32).reshape(R, CW).astype(BF16) for c in range(NC)]
    latent = jnp.zeros((R, L), F32)
    for c in range(NC):
        latent = latent + dot(pieces[c], wd[c * CW : (c + 1) * CW, :])
    mine = pl.ds(pl.multiple_of(me * L, L), L)
    lat_all[blk, mine] = latent.astype(BF16)

    def lat_copy(i):
        return pltpu.make_async_remote_copy(
            src_ref=lat_all.at[blk, mine],
            dst_ref=lat_all.at[blk, mine],
            send_sem=s3.at[i - 1],
            recv_sem=r3.at[i - 1],
            device_id={"ep": ep_peer(i)},
            device_id_type=MESH,
        )

    def w_copy(i):
        return pltpu.make_async_remote_copy(
            src_ref=w_all.at[ep],
            dst_ref=w_all.at[ep],
            send_sem=s3w.at[i - 1],
            recv_sem=r3w.at[i - 1],
            device_id={"ep": ep_peer(i)},
            device_id_type=MESH,
        )

    def fwd_copy(i, k):
        rows = pl.ds(pl.multiple_of(ep_peer(E - i) * R, R), R)
        return pltpu.make_async_remote_copy(
            src_ref=lat_all.at[rows, mine],
            dst_ref=lat_all.at[rows, mine],
            send_sem=s4.at[i, k - 1],
            recv_sem=r4.at[i, k - 1],
            device_id={"tp": tp_peer(k)},
            device_id_type=MESH,
        )

    for i in range(1, E):
        lat_copy(i).start()
    for k in range(1, T):
        fwd_copy(0, k).start()

    logits = jnp.zeros((R, XA), F32)
    for c in range(NC):
        logits = logits + dot(pieces[c], router[c * CW : (c + 1) * CW, :])
    gates = jax.nn.sigmoid(logits)
    w_all[ep] = kept * gates / jnp.sum(picked * gates, axis=-1, keepdims=True)
    for i in range(1, E):
        w_copy(i).start()

    for i in range(1, E):
        lat_copy(i).wait_recv()
        for k in range(1, T):
            fwd_copy(i, k).start()
    for i in range(1, E):
        w_copy(i).wait_recv()
    for i in range(E):
        for k in range(1, T):
            fwd_copy(i, k).wait_recv()

    BR = 128 if N % 128 == 0 else R
    NB = N // BR
    per = BR // R
    for load in loads[3:]:
        load.wait()

    def expert(x, carry):
        def rows_step(b, carry):
            rows = pl.ds(pl.multiple_of(b * BR, BR), BR)
            lat = lat_all[rows, :]
            gate = dot(lat, wg[x])
            upper = dot(lat, wp[x])
            weights = w_all[pl.ds(b * per, per)].reshape(BR, XA)
            lane = lax.broadcasted_iota(jnp.int32, (BR, XA), 1)
            scaled = jnp.sum(
                jnp.where(lane == ep * X + x, weights, 0.0), axis=-1, keepdims=True
            )
            act[x, rows] = (jax.nn.silu(gate) * upper * scaled).astype(BF16)
            return carry

        return lax.fori_loop(0, NB, rows_step, carry)

    lax.fori_loop(0, X, expert, 0)

    def c_copy(k):
        return pltpu.make_async_remote_copy(
            src_ref=c_send.at[k - 1],
            dst_ref=c_recv.at[k - 1],
            send_sem=s5.at[k - 1],
            recv_sem=r5.at[k - 1],
            device_id={"tp": tp_peer(k)},
            device_id_type=MESH,
        )

    def down(k, b):
        rows = pl.ds(pl.multiple_of(b * BR, BR), BR)
        cols = pl.ds(pl.multiple_of(tp_peer(k) * L, L), L)
        value = dot(act[0, rows], wn[0, :, cols])
        for x in range(1, X):
            value = value + dot(act[x, rows], wn[x, :, cols])
        return rows, value

    for k in range(1, T):

        def send_rows(b, carry):
            rows, value = down(k, b)
            c_send[k - 1, rows] = value.astype(BF16)
            return carry

        lax.fori_loop(0, NB, send_rows, 0)
        c_copy(k).start()

    def own_rows(b, carry):
        rows, value = down(T, b)
        c_own[rows, :] = value
        return carry

    lax.fori_loop(0, NB, own_rows, 0)
    for k in range(1, T):
        c_copy(k).wait_recv()

    def d_copy(i):
        return pltpu.make_async_remote_copy(
            src_ref=d_send.at[ep_peer(i)],
            dst_ref=d_recv.at[i - 1],
            send_sem=s6.at[i - 1],
            recv_sem=r6.at[i - 1],
            device_id={"ep": ep_peer(i)},
            device_id_type=MESH,
        )

    def block_sum(j):
        rows = pl.ds(pl.multiple_of(j * R, R), R)
        value = c_own[rows, :]
        for k in range(1, T):
            value = value + c_recv[k - 1, rows].astype(F32)
        return value

    for i in range(1, E):
        d_send[ep_peer(i)] = block_sum(ep_peer(i)).astype(BF16)
        d_copy(i).start()
    combined = block_sum(ep)
    for i in range(1, E):
        d_copy(i).wait_recv()
        combined = combined + d_recv[i - 1].astype(F32)
    combined = combined.astype(BF16)

    def l_copy(c, k):
        peer = tp_peer(k)
        return pltpu.make_async_remote_copy(
            src_ref=l_send.at[c, peer],
            dst_ref=l_recv.at[c, k - 1],
            send_sem=s7.at[c, k - 1],
            recv_sem=r7.at[c, k - 1],
            device_id={"tp": peer},
            device_id_type=MESH,
        )

    def lift(c, carry):
        cols = pl.ds(pl.multiple_of(c * CW, CW), CW)
        part = dot(combined, wu[:, cols]).reshape(T, r, CW)
        l_own[c] = part
        l_send[c] = part.astype(BF16)
        for k in range(1, T):
            l_copy(c, k).start()
        return carry

    lax.fori_loop(0, NC, lift, 0)
    for c in range(NC):
        value = res[c] + l_own[c, me]
        for k in range(1, T):
            l_copy(c, k).wait_recv()
            value = value + l_recv[c, k - 1].astype(F32)
        out_ref[:, c * CW : (c + 1) * CW] = value.astype(BF16)

    for k in range(1, T):
        n_copy(k).wait_send()
        c_copy(k).wait_send()
        for c in range(NC):
            p_copy(c, k).wait_send()
            l_copy(c, k).wait_send()
        for i in range(E):
            fwd_copy(i, k).wait_send()
    for i in range(1, E):
        lat_copy(i).wait_send()
        w_copy(i).wait_send()
        d_copy(i).wait_send()


def on_device(
    hidden_in,
    queries,
    new_keys,
    new_values,
    key_cache,
    value_cache,
    lengths,
    out_weight,
    norm_gain,
    router_weight,
    latent_down,
    latent_up,
    gate_weight,
    up_weight,
    down_weight,
    routes,
    slot_index,
):
    T = lax.axis_size("tp")
    E = lax.axis_size("ep")
    R, Hl, HD = queries.shape
    D = hidden_in.shape[1]
    r = R // T
    L = latent_down.shape[1]
    LAT = L * T
    X, _, F = gate_weight.shape
    XA = router_weight.shape[1]
    N, TOPK = routes.shape
    slots_all = 2 * N * TOPK // XA
    NC = 4
    CW = D // NC
    dims = (T, E, R, r, D, NC, L, X, XA, F, N, TOPK, slots_all)
    vmem = pl.BlockSpec(memory_space=pltpu.VMEM)
    smem = pl.BlockSpec(memory_space=pltpu.SMEM)
    hbm = pl.BlockSpec(memory_space=pl.ANY)
    dma = pltpu.SemaphoreType.DMA
    scratch = [
        pltpu.VMEM(key_cache.shape, BF16),
        pltpu.VMEM(value_cache.shape, BF16),
        pltpu.VMEM(out_weight.shape, BF16),
        pltpu.VMEM(router_weight.shape, BF16),
        pltpu.VMEM(latent_down.shape, BF16),
        pltpu.VMEM(latent_up.shape, BF16),
        pltpu.VMEM(gate_weight.shape, BF16),
        pltpu.VMEM(up_weight.shape, BF16),
        pltpu.VMEM(down_weight.shape, BF16),
        pltpu.VMEM((r, D), BF16),
        pltpu.VMEM((R, Hl, HD), F32),
        pltpu.VMEM((NC, T, r, CW), F32),
        pltpu.VMEM((NC, T, r, CW), BF16),
        pltpu.VMEM((NC, T - 1, r, CW), BF16),
        pltpu.VMEM((NC, r, CW), F32),
        pltpu.VMEM((T, NC, r, CW), BF16),
        pltpu.VMEM((N, LAT), BF16),
        pltpu.VMEM((E, R, XA), F32),
        pltpu.VMEM((X, N, F), BF16),
        pltpu.VMEM((N, L), F32),
        pltpu.VMEM((T - 1, N, L), BF16),
        pltpu.VMEM((T - 1, N, L), BF16),

        pltpu.VMEM((E, R, L), BF16),
        pltpu.VMEM((E - 1, R, L), BF16),
        pltpu.VMEM((NC, T, r, CW), F32),
        pltpu.VMEM((NC, T, r, CW), BF16),
        pltpu.VMEM((NC, T - 1, r, CW), BF16),
        dma((2, R // 8)),
        dma((8,)),
        dma((NC, T - 1)),
        dma((NC, T - 1)),
        dma((T - 1,)),
        dma((T - 1,)),
        dma((E - 1,)),
        dma((E - 1,)),
        dma((E - 1,)),
        dma((E - 1,)),
        dma((E, T - 1)),
        dma((E, T - 1)),
        dma((T - 1,)),
        dma((T - 1,)),
        dma((E - 1,)),
        dma((E - 1,)),
        dma((NC, T - 1)),
        dma((NC, T - 1)),
    ]
    return pl.pallas_call(
        functools.partial(layer_kernel, dims),
        out_shape=jax.ShapeDtypeStruct((r, D), BF16),
        in_specs=[
            hbm,
            vmem,
            vmem,
            vmem,
            hbm,
            hbm,
            smem,
            hbm,
            vmem,
            hbm,
            hbm,
            hbm,
            hbm,
            hbm,
            hbm,
            vmem,
            vmem,
        ],
        out_specs=vmem,
        scratch_shapes=scratch,
        compiler_params=pltpu.CompilerParams(
            collective_id=0, has_side_effects=True, vmem_limit_bytes=60 * 1024 * 1024
        ),
    )(
        hidden_in.reshape(T, r, D),
        queries,
        new_keys,
        new_values,
        key_cache,
        value_cache,
        lengths,
        out_weight,
        norm_gain.reshape(1, D),
        router_weight,
        latent_down,
        latent_up,
        gate_weight,
        up_weight,
        down_weight,
        routes,
        slot_index,
    )


def solution(mesh):
    return jax.shard_map(
        on_device,
        mesh=mesh,
        in_specs=(
            P(("rep", "ep"), None),
            P(("rep", "ep"), "tp", None),
            P(("rep", "ep"), "tp", None),
            P(("rep", "ep"), "tp", None),
            P(("rep", "ep"), "tp", None, None),
            P(("rep", "ep"), "tp", None, None),
            P(("rep", "ep")),
            P("tp", None),
            P(),
            P(),
            P(None, "tp"),
            P("tp", None),
            P("ep", None, "tp"),
            P("ep", None, "tp"),
            P("ep", "tp", None),
            P("rep", None),
            P("rep", None),
        ),
        out_specs=P(("rep", "ep", "tp"), None),
        check_vma=False,
    )
```

```python
import functools
import math

import jax
import jax.numpy as jnp
from jax import lax
from jax.experimental import pallas as pl
from jax.experimental.pallas import tpu as pltpu
from jax.sharding import PartitionSpec as P

MESH = pl.DeviceIdType.MESH
F32 = jnp.float32
BF16 = jnp.bfloat16


def dot(a, b):
    return jnp.dot(a, b, preferred_element_type=F32)


def dot_nt(a, b):
    return lax.dot_general(a, b, (((1,), (1,)), ((), ())), preferred_element_type=F32)


def layer_kernel(
    dims,
    hidden_ref,
    q_ref,
    nk_ref,
    nv_ref,
    k_hbm,
    v_hbm,
    len_ref,
    wo_hbm,
    gain_ref,
    router_hbm,
    wd_hbm,
    wu_hbm,
    wg_hbm,
    wp_hbm,
    wn_hbm,
    routes_ref,
    slots_ref,
    out_ref,
    kbuf,
    vbuf,
    wo,
    router,
    wd,
    wu,
    wg,
    wp,
    wn,
    hid,
    att,
    p_own,
    p_send,
    p_recv,
    res,
    n_all,
    lat_all,
    lat_mat,
    w_all,
    picked_all,
    kept_all,
    act,
    c_own,
    c_send,
    c_recv,
    d_send,
    d_recv,
    l_own,
    l_send,
    l_recv,
    kv_sem,
    w_sem,
    s1,
    r1,
    s2,
    r2,
    s3,
    r3,
    s3w,
    r3w,
    s4,
    r4,
    s5,
    r5,
    s6,
    r6,
    s7,
    r7,
):
    (T, E, R, r, D, NC, L, X, XA, F, N, TOPK, slots_all) = dims
    me = lax.axis_index("tp")
    ep = lax.axis_index("ep")
    CW = D // NC
    Hl, HD = q_ref.shape[1], q_ref.shape[2]
    G = nk_ref.shape[1]
    grp = Hl // G
    CACHE = k_hbm.shape[2]
    AC = 8
    NA = R // AC

    def tp_peer(k):
        return lax.rem(me + k, T)

    def ep_peer(i):
        return lax.rem(ep + i, E)

    def kv_copy(c, which):
        src, dst = ((k_hbm, kbuf), (v_hbm, vbuf))[which]
        rows = pl.ds(c * AC, AC)
        return pltpu.make_async_copy(src.at[rows], dst.at[rows], kv_sem.at[which, c])

    for c in range(NA):
        kv_copy(c, 0).start()
        kv_copy(c, 1).start()
    hid_copy = pltpu.make_async_copy(hidden_ref.at[me], hid, w_sem.at[0])
    loads = [
        pltpu.make_async_copy(src, dst, w_sem.at[i + 1])
        for i, (src, dst) in enumerate(
            (
                (wo_hbm, wo),
                (wd_hbm, wd),
                (router_hbm, router),
                (wg_hbm, wg),
                (wp_hbm, wp),
                (wn_hbm, wn),
                (wu_hbm, wu),
            )
        )
    ]
    loads[0].start()
    hid_copy.start()

    barrier = pltpu.get_barrier_semaphore()
    for k in range(1, T):
        pl.semaphore_signal(barrier, inc=1, device_id={"tp": tp_peer(k)}, device_id_type=MESH)
    for i in range(1, E):
        pl.semaphore_signal(barrier, inc=1, device_id={"ep": ep_peer(i)}, device_id_type=MESH)

    for load in loads[1:]:
        load.start()

    scale = 1.0 / math.sqrt(HD)

    def by_group(pieces, width):
        row = lax.broadcasted_iota(jnp.int32, (Hl, width), 0)
        value = jnp.broadcast_to(pieces[0], (Hl, width))
        for g in range(1, G):
            value = jnp.where(row >= g * grp, jnp.broadcast_to(pieces[g], (Hl, width)), value)
        return value

    def attend(c, carry):
        kv_copy(c, 0).wait()
        scores, owns = [], []
        column = lax.broadcasted_iota(jnp.int32, (Hl, CACHE), 1)
        for i in range(AC):
            s = c * AC + i
            qs = q_ref[s]
            sc = by_group([dot_nt(qs, kbuf[s, g]) for g in range(G)], CACHE) * scale
            scores.append(jnp.where(column < len_ref[s], sc, -jnp.inf))
            nks = nk_ref[s].astype(F32)
            nkx = by_group([nks[g : g + 1] for g in range(G)], HD)
            owns.append(jnp.sum(qs.astype(F32) * nkx, axis=-1, keepdims=True) * scale)
        kv_copy(c, 1).wait()
        probs, own_probs = [], []
        for i in range(AC):
            top = jnp.maximum(jnp.max(scores[i], axis=-1, keepdims=True), owns[i])
            expo = jnp.exp(scores[i] - top)
            own_expo = jnp.exp(owns[i] - top)
            total = jnp.sum(expo, axis=-1, keepdims=True) + own_expo
            probs.append((expo / total).astype(BF16))
            own_probs.append((own_expo / total).astype(BF16).astype(F32))
        for i in range(AC):
            s = c * AC + i
            mixed = by_group([dot(probs[i], vbuf[s, g]) for g in range(G)], HD)
            nvs = nv_ref[s].astype(F32)
            nvx = by_group([nvs[g : g + 1] for g in range(G)], HD)
            att[s] = mixed + own_probs[i] * nvx
        return carry

    lax.fori_loop(0, NA, attend, 0)
    attended = jnp.concatenate([att[:, h, :] for h in range(Hl)], axis=1).astype(BF16)

    pl.semaphore_wait(barrier, T - 1 + E - 1)

    def p_copy(c, k):
        peer = tp_peer(k)
        return pltpu.make_async_remote_copy(
            src_ref=p_send.at[c, peer],
            dst_ref=p_recv.at[c, k - 1],
            send_sem=s1.at[c, k - 1],
            recv_sem=r1.at[c, k - 1],
            device_id={"tp": peer},
            device_id_type=MESH,
        )

    loads[0].wait()

    def project(c, carry):
        cols = pl.ds(pl.multiple_of(c * CW, CW), CW)
        part = dot(attended, wo[:, cols]).reshape(T, r, CW)
        p_own[c] = part
        p_send[c] = part.astype(BF16)
        for k in range(1, T):
            p_copy(c, k).start()
        return carry

    lax.fori_loop(0, NC, project, 0)

    ident = lax.broadcasted_iota(jnp.int32, (XA, N), 0)
    picked = jnp.zeros((XA, N), F32)
    kept = jnp.zeros((XA, N), F32)
    for k in range(TOPK):
        hit = jnp.where(routes_ref[k : k + 1, :] == ident, 1.0, 0.0)
        picked = picked + hit
        kept = kept + jnp.where(slots_ref[k : k + 1, :] < slots_all, hit, 0.0)
    picked_all[...] = picked.T
    kept_all[...] = kept.T

    hid_copy.wait()
    sumsq = jnp.zeros((r, 1), F32)
    for c in range(NC):
        value = hid[:, c * CW : (c + 1) * CW].astype(F32) + p_own[c, me]
        for k in range(1, T):
            p_copy(c, k).wait_recv()
            value = value + p_recv[c, k - 1].astype(F32)
        res[c] = value
        sumsq = sumsq + jnp.sum(value * value, axis=-1, keepdims=True)
    inv = lax.rsqrt(sumsq * (1.0 / D) + 1e-05)
    for c in range(NC):
        gain = gain_ref[c * CW : (c + 1) * CW].astype(F32).reshape(1, CW)
        n_all[me, c] = (res[c] * inv * gain).astype(BF16)

    def n_copy(k):
        peer = tp_peer(k)
        return pltpu.make_async_remote_copy(
            src_ref=n_all.at[me],
            dst_ref=n_all.at[me],
            send_sem=s2.at[k - 1],
            recv_sem=r2.at[k - 1],
            device_id={"tp": peer},
            device_id_type=MESH,
        )

    for k in range(1, T):
        n_copy(k).start()

    blk = pl.ds(pl.multiple_of(ep * R, R), R)
    picked = picked_all[blk, :]
    kept = kept_all[blk, :]

    loads[1].wait()
    loads[2].wait()
    for k in range(1, T):
        n_copy(k).wait_recv()
    pieces = [n_all[:, c].astype(F32).reshape(R, CW).astype(BF16) for c in range(NC)]
    latent = jnp.zeros((R, L), F32)
    for c in range(NC):
        latent = latent + dot(pieces[c], wd[c * CW : (c + 1) * CW, :])
    lat_all[me, ep] = latent.astype(BF16)

    def lat_copy(i):
        return pltpu.make_async_remote_copy(
            src_ref=lat_all.at[me, ep],
            dst_ref=lat_all.at[me, ep],
            send_sem=s3.at[i - 1],
            recv_sem=r3.at[i - 1],
            device_id={"ep": ep_peer(i)},
            device_id_type=MESH,
        )

    def w_copy(i):
        return pltpu.make_async_remote_copy(
            src_ref=w_all.at[ep],
            dst_ref=w_all.at[ep],
            send_sem=s3w.at[i - 1],
            recv_sem=r3w.at[i - 1],
            device_id={"ep": ep_peer(i)},
            device_id_type=MESH,
        )

    def fwd_copy(i, k):
        row = ep_peer(E - i)
        return pltpu.make_async_remote_copy(
            src_ref=lat_all.at[me, row],
            dst_ref=lat_all.at[me, row],
            send_sem=s4.at[i, k - 1],
            recv_sem=r4.at[i, k - 1],
            device_id={"tp": tp_peer(k)},
            device_id_type=MESH,
        )

    for i in range(1, E):
        lat_copy(i).start()
    for k in range(1, T):
        fwd_copy(0, k).start()

    logits = jnp.zeros((R, XA), F32)
    for c in range(NC):
        logits = logits + dot_nt(pieces[c], router[:, c * CW : (c + 1) * CW])
    gates = jax.nn.sigmoid(logits)
    w_all[ep] = kept * gates / jnp.sum(picked * gates, axis=-1, keepdims=True)
    for i in range(1, E):
        w_copy(i).start()

    for i in range(1, E):
        lat_copy(i).wait_recv()
        for k in range(1, T):
            fwd_copy(i, k).start()
    for i in range(1, E):
        w_copy(i).wait_recv()
    for i in range(E):
        for k in range(1, T):
            fwd_copy(i, k).wait_recv()

    BR = 128 if N % 128 == 0 else R
    NB = N // BR
    per = BR // R
    for load in loads[3:]:
        load.wait()

    for t in range(T):
        lat_mat[:, t * L : (t + 1) * L] = lat_all[t].reshape(N, L)

    def expert(x, carry):
        def rows_step(b, carry):
            rows = pl.ds(pl.multiple_of(b * BR, BR), BR)
            lat = lat_mat[rows, :]
            gate = dot(lat, wg[x])
            upper = dot(lat, wp[x])
            weights = w_all[pl.ds(b * per, per)].reshape(BR, XA)
            lane = lax.broadcasted_iota(jnp.int32, (BR, XA), 1)
            scaled = jnp.sum(
                jnp.where(lane == ep * X + x, weights, 0.0), axis=-1, keepdims=True
            )
            act[x, rows] = (jax.nn.silu(gate) * upper * scaled).astype(BF16)
            return carry

        return lax.fori_loop(0, NB, rows_step, carry)

    lax.fori_loop(0, X, expert, 0)

    def c_copy(k):
        return pltpu.make_async_remote_copy(
            src_ref=c_send.at[k - 1],
            dst_ref=c_recv.at[k - 1],
            send_sem=s5.at[k - 1],
            recv_sem=r5.at[k - 1],
            device_id={"tp": tp_peer(k)},
            device_id_type=MESH,
        )

    def down(k, b):
        rows = pl.ds(pl.multiple_of(b * BR, BR), BR)
        cols = pl.ds(pl.multiple_of(tp_peer(k) * L, L), L)
        value = dot(act[0, rows], wn[0, :, cols])
        for x in range(1, X):
            value = value + dot(act[x, rows], wn[x, :, cols])
        return rows, value

    for k in range(1, T):

        def send_rows(b, carry):
            rows, value = down(k, b)
            c_send[k - 1, rows] = value.astype(BF16)
            return carry

        lax.fori_loop(0, NB, send_rows, 0)
        c_copy(k).start()

    def own_rows(b, carry):
        rows, value = down(T, b)
        c_own[rows, :] = value
        return carry

    lax.fori_loop(0, NB, own_rows, 0)
    for k in range(1, T):
        c_copy(k).wait_recv()

    def d_copy(i):
        return pltpu.make_async_remote_copy(
            src_ref=d_send.at[ep_peer(i)],
            dst_ref=d_recv.at[i - 1],
            send_sem=s6.at[i - 1],
            recv_sem=r6.at[i - 1],
            device_id={"ep": ep_peer(i)},
            device_id_type=MESH,
        )

    def block_sum(j):
        rows = pl.ds(pl.multiple_of(j * R, R), R)
        value = c_own[rows, :]
        for k in range(1, T):
            value = value + c_recv[k - 1, rows].astype(F32)
        return value

    for i in range(1, E):
        d_send[ep_peer(i)] = block_sum(ep_peer(i)).astype(BF16)
        d_copy(i).start()
    combined = block_sum(ep)
    for i in range(1, E):
        d_copy(i).wait_recv()
        combined = combined + d_recv[i - 1].astype(F32)
    combined = combined.astype(BF16)

    def l_copy(c, k):
        peer = tp_peer(k)
        return pltpu.make_async_remote_copy(
            src_ref=l_send.at[c, peer],
            dst_ref=l_recv.at[c, k - 1],
            send_sem=s7.at[c, k - 1],
            recv_sem=r7.at[c, k - 1],
            device_id={"tp": peer},
            device_id_type=MESH,
        )

    def lift(c, carry):
        cols = pl.ds(pl.multiple_of(c * CW, CW), CW)
        part = dot(combined, wu[:, cols]).reshape(T, r, CW)
        l_own[c] = part
        l_send[c] = part.astype(BF16)
        for k in range(1, T):
            l_copy(c, k).start()
        return carry

    lax.fori_loop(0, NC, lift, 0)
    for c in range(NC):
        value = res[c] + l_own[c, me]
        for k in range(1, T):
            l_copy(c, k).wait_recv()
            value = value + l_recv[c, k - 1].astype(F32)
        out_ref[:, c * CW : (c + 1) * CW] = value.astype(BF16)

    for k in range(1, T):
        n_copy(k).wait_send()
        c_copy(k).wait_send()
        for c in range(NC):
            p_copy(c, k).wait_send()
            l_copy(c, k).wait_send()
        for i in range(E):
            fwd_copy(i, k).wait_send()
    for i in range(1, E):
        lat_copy(i).wait_send()
        w_copy(i).wait_send()
        d_copy(i).wait_send()


def on_device(
    hidden_in,
    queries,
    new_keys,
    new_values,
    key_cache,
    value_cache,
    lengths,
    out_weight,
    norm_gain,
    router_weight,
    latent_down,
    latent_up,
    gate_weight,
    up_weight,
    down_weight,
    routes,
    slot_index,
):
    T = lax.axis_size("tp")
    E = lax.axis_size("ep")
    R, Hl, HD = queries.shape
    D = hidden_in.shape[1]
    r = R // T
    L = latent_down.shape[1]
    LAT = L * T
    X, _, F = gate_weight.shape
    XA = router_weight.shape[1]
    N, TOPK = routes.shape
    slots_all = 2 * N * TOPK // XA
    NC = 4
    CW = D // NC
    dims = (T, E, R, r, D, NC, L, X, XA, F, N, TOPK, slots_all)
    vmem = pl.BlockSpec(memory_space=pltpu.VMEM)
    smem = pl.BlockSpec(memory_space=pltpu.SMEM)
    hbm = pl.BlockSpec(memory_space=pl.ANY)
    dma = pltpu.SemaphoreType.DMA
    scratch = [
        pltpu.VMEM(key_cache.shape, BF16),
        pltpu.VMEM(value_cache.shape, BF16),
        pltpu.VMEM(out_weight.shape, BF16),
        pltpu.VMEM((XA, D), BF16),
        pltpu.VMEM(latent_down.shape, BF16),
        pltpu.VMEM(latent_up.shape, BF16),
        pltpu.VMEM(gate_weight.shape, BF16),
        pltpu.VMEM(up_weight.shape, BF16),
        pltpu.VMEM(down_weight.shape, BF16),
        pltpu.VMEM((r, D), BF16),
        pltpu.VMEM((R, Hl, HD), F32),
        pltpu.VMEM((NC, T, r, CW), F32),
        pltpu.VMEM((NC, T, r, CW), BF16),
        pltpu.VMEM((NC, T - 1, r, CW), BF16),
        pltpu.VMEM((NC, r, CW), F32),
        pltpu.VMEM((T, NC, r, CW), BF16),
        pltpu.VMEM((T, E, R, L), BF16),
        pltpu.VMEM((N, LAT), BF16),
        pltpu.VMEM((E, R, XA), F32),
        pltpu.VMEM((N, XA), F32),
        pltpu.VMEM((N, XA), F32),
        pltpu.VMEM((X, N, F), BF16),
        pltpu.VMEM((N, L), F32),
        pltpu.VMEM((T - 1, N, L), BF16),
        pltpu.VMEM((T - 1, N, L), BF16),

        pltpu.VMEM((E, R, L), BF16),
        pltpu.VMEM((E - 1, R, L), BF16),
        pltpu.VMEM((NC, T, r, CW), F32),
        pltpu.VMEM((NC, T, r, CW), BF16),
        pltpu.VMEM((NC, T - 1, r, CW), BF16),
        dma((2, R // 8)),
        dma((8,)),
        dma((NC, T - 1)),
        dma((NC, T - 1)),
        dma((T - 1,)),
        dma((T - 1,)),
        dma((E - 1,)),
        dma((E - 1,)),
        dma((E - 1,)),
        dma((E - 1,)),
        dma((E, T - 1)),
        dma((E, T - 1)),
        dma((T - 1,)),
        dma((T - 1,)),
        dma((E - 1,)),
        dma((E - 1,)),
        dma((NC, T - 1)),
        dma((NC, T - 1)),
    ]
    return pl.pallas_call(
        functools.partial(layer_kernel, dims),
        out_shape=jax.ShapeDtypeStruct((r, D), BF16),
        in_specs=[
            hbm,
            vmem,
            vmem,
            vmem,
            hbm,
            hbm,
            smem,
            hbm,
            vmem,
            hbm,
            hbm,
            hbm,
            hbm,
            hbm,
            hbm,
            vmem,
            vmem,
        ],
        out_specs=vmem,
        scratch_shapes=scratch,
        compiler_params=pltpu.CompilerParams(
            collective_id=0, has_side_effects=True, vmem_limit_bytes=60 * 1024 * 1024
        ),
    )(
        hidden_in.reshape(T, r, D),
        queries,
        new_keys,
        new_values,
        key_cache,
        value_cache,
        lengths,
        out_weight,
        norm_gain,
        router_weight.T,
        latent_down,
        latent_up,
        gate_weight,
        up_weight,
        down_weight,
        routes.T,
        slot_index.T,
    )


def solution(mesh):
    return jax.shard_map(
        on_device,
        mesh=mesh,
        in_specs=(
            P(("rep", "ep"), None),
            P(("rep", "ep"), "tp", None),
            P(("rep", "ep"), "tp", None),
            P(("rep", "ep"), "tp", None),
            P(("rep", "ep"), "tp", None, None),
            P(("rep", "ep"), "tp", None, None),
            P(("rep", "ep")),
            P("tp", None),
            P(),
            P(),
            P(None, "tp"),
            P("tp", None),
            P("ep", None, "tp"),
            P("ep", None, "tp"),
            P("ep", "tp", None),
            P("rep", None),
            P("rep", None),
        ),
        out_specs=P(("rep", "ep", "tp"), None),
        check_vma=False,
    )
```

```python
import functools
import math

import jax
import jax.numpy as jnp
from jax import lax
from jax.experimental import pallas as pl
from jax.experimental.pallas import tpu as pltpu
from jax.sharding import PartitionSpec as P

MESH = pl.DeviceIdType.MESH
F32 = jnp.float32
BF16 = jnp.bfloat16


def dot(a, b):
    return jnp.dot(a, b, preferred_element_type=F32)


def dot_nt(a, b):
    return lax.dot_general(a, b, (((1,), (1,)), ((), ())), preferred_element_type=F32)


def layer_kernel(
    dims,
    hidden_ref,
    q_ref,
    nk_ref,
    nv_ref,
    k_hbm,
    v_hbm,
    len_ref,
    wo_hbm,
    gain_ref,
    router_hbm,
    wd_hbm,
    wu_hbm,
    wg_hbm,
    wp_hbm,
    wn_hbm,
    routes_ref,
    slots_ref,
    out_ref,
    kbuf,
    vbuf,
    wo,
    router,
    wd,
    wu,
    wg,
    wp,
    wn,
    hid,
    att,
    p_own,
    p_send,
    p_recv,
    res,
    n_all,
    lat_all,
    lat_mat,
    w_all,
    picked_all,
    kept_all,
    act,
    c_own,
    c_send,
    c_recv,
    d_send,
    d_recv,
    l_own,
    l_send,
    l_recv,
    kv_sem,
    w_sem,
    s1,
    r1,
    s2,
    r2,
    s3,
    r3,
    s3w,
    r3w,
    s4,
    r4,
    s5,
    r5,
    s6,
    r6,
    s7,
    r7,
):
    (T, E, R, r, D, NC, L, X, XA, F, N, TOPK, slots_all) = dims
    me = lax.axis_index("tp")
    ep = lax.axis_index("ep")
    CW = D // NC
    Hl, HD = q_ref.shape[1], q_ref.shape[2]
    G = nk_ref.shape[1]
    grp = Hl // G
    CACHE = k_hbm.shape[2]
    AC = 8
    NA = R // AC

    def tp_peer(k):
        return lax.rem(me + k, T)

    def ep_peer(i):
        return lax.rem(ep + i, E)

    def kv_copy(c, which):
        src, dst = ((k_hbm, kbuf), (v_hbm, vbuf))[which]
        rows = pl.ds(c * AC, AC)
        return pltpu.make_async_copy(src.at[rows], dst.at[rows], kv_sem.at[which, c])

    for c in range(NA):
        kv_copy(c, 0).start()
        kv_copy(c, 1).start()
    hid_copy = pltpu.make_async_copy(hidden_ref.at[me], hid, w_sem.at[0])
    loads = [
        pltpu.make_async_copy(src, dst, w_sem.at[i + 1])
        for i, (src, dst) in enumerate(
            (
                (wo_hbm, wo),
                (wd_hbm, wd),
                (router_hbm, router),
                (wg_hbm, wg),
                (wp_hbm, wp),
                (wn_hbm, wn),
                (wu_hbm, wu),
            )
        )
    ]
    loads[0].start()
    hid_copy.start()

    barrier = pltpu.get_barrier_semaphore()
    for k in range(1, T):
        pl.semaphore_signal(barrier, inc=1, device_id={"tp": tp_peer(k)}, device_id_type=MESH)
    for i in range(1, E):
        pl.semaphore_signal(barrier, inc=1, device_id={"ep": ep_peer(i)}, device_id_type=MESH)

    for load in loads[1:]:
        load.start()

    far_first = sorted(range(1, T), key=lambda k: abs(2 * k - T))
    scale = 1.0 / math.sqrt(HD)

    def by_group(pieces, width):
        row = lax.broadcasted_iota(jnp.int32, (Hl, width), 0)
        value = jnp.broadcast_to(pieces[0], (Hl, width))
        for g in range(1, G):
            value = jnp.where(row >= g * grp, jnp.broadcast_to(pieces[g], (Hl, width)), value)
        return value

    def attend(c, carry):
        kv_copy(c, 0).wait()
        scores, owns = [], []
        column = lax.broadcasted_iota(jnp.int32, (Hl, CACHE), 1)
        for i in range(AC):
            s = c * AC + i
            qs = q_ref[s]
            sc = by_group([dot_nt(qs, kbuf[s, g]) for g in range(G)], CACHE) * scale
            scores.append(jnp.where(column < len_ref[s], sc, -jnp.inf))
            nks = nk_ref[s].astype(F32)
            nkx = by_group([nks[g : g + 1] for g in range(G)], HD)
            owns.append(jnp.sum(qs.astype(F32) * nkx, axis=-1, keepdims=True) * scale)
        kv_copy(c, 1).wait()
        probs, own_probs = [], []
        for i in range(AC):
            top = jnp.maximum(jnp.max(scores[i], axis=-1, keepdims=True), owns[i])
            expo = jnp.exp(scores[i] - top)
            own_expo = jnp.exp(owns[i] - top)
            total = jnp.sum(expo, axis=-1, keepdims=True) + own_expo
            probs.append((expo / total).astype(BF16))
            own_probs.append((own_expo / total).astype(BF16).astype(F32))
        for i in range(AC):
            s = c * AC + i
            mixed = by_group([dot(probs[i], vbuf[s, g]) for g in range(G)], HD)
            nvs = nv_ref[s].astype(F32)
            nvx = by_group([nvs[g : g + 1] for g in range(G)], HD)
            att[s] = mixed + own_probs[i] * nvx
        return carry

    lax.fori_loop(0, NA, attend, 0)
    attended = jnp.concatenate([att[:, h, :] for h in range(Hl)], axis=1).astype(BF16)

    pl.semaphore_wait(barrier, T - 1 + E - 1)

    def p_copy(c, k):
        peer = tp_peer(k)
        return pltpu.make_async_remote_copy(
            src_ref=p_send.at[c, peer],
            dst_ref=p_recv.at[c, k - 1],
            send_sem=s1.at[c, k - 1],
            recv_sem=r1.at[c, k - 1],
            device_id={"tp": peer},
            device_id_type=MESH,
        )

    loads[0].wait()

    def project(c, carry):
        cols = pl.ds(pl.multiple_of(c * CW, CW), CW)
        part = dot(attended, wo[:, cols]).reshape(T, r, CW)
        p_own[c] = part
        p_send[c] = part.astype(BF16)
        for k in far_first:
            p_copy(c, k).start()
        return carry

    lax.fori_loop(0, NC, project, 0)

    ident = lax.broadcasted_iota(jnp.int32, (XA, N), 0)
    picked = jnp.zeros((XA, N), F32)
    kept = jnp.zeros((XA, N), F32)
    for k in range(TOPK):
        hit = jnp.where(routes_ref[k : k + 1, :] == ident, 1.0, 0.0)
        picked = picked + hit
        kept = kept + jnp.where(slots_ref[k : k + 1, :] < slots_all, hit, 0.0)
    picked_all[...] = picked.T
    kept_all[...] = kept.T

    hid_copy.wait()
    sumsq = jnp.zeros((r, 1), F32)
    for c in range(NC):
        value = hid[:, c * CW : (c + 1) * CW].astype(F32) + p_own[c, me]
        for k in range(1, T):
            p_copy(c, k).wait_recv()
            value = value + p_recv[c, k - 1].astype(F32)
        res[c] = value
        sumsq = sumsq + jnp.sum(value * value, axis=-1, keepdims=True)
    inv = lax.rsqrt(sumsq * (1.0 / D) + 1e-05)
    for c in range(NC):
        gain = gain_ref[c * CW : (c + 1) * CW].astype(F32).reshape(1, CW)
        n_all[me, c] = (res[c] * inv * gain).astype(BF16)

    def n_copy(k):
        peer = tp_peer(k)
        return pltpu.make_async_remote_copy(
            src_ref=n_all.at[me],
            dst_ref=n_all.at[me],
            send_sem=s2.at[k - 1],
            recv_sem=r2.at[k - 1],
            device_id={"tp": peer},
            device_id_type=MESH,
        )

    for k in far_first:
        n_copy(k).start()

    blk = pl.ds(pl.multiple_of(ep * R, R), R)
    picked = picked_all[blk, :]
    kept = kept_all[blk, :]

    loads[1].wait()
    loads[2].wait()
    for k in range(1, T):
        n_copy(k).wait_recv()
    pieces = [n_all[:, c].astype(F32).reshape(R, CW).astype(BF16) for c in range(NC)]
    latent = jnp.zeros((R, L), F32)
    for c in range(NC):
        latent = latent + dot(pieces[c], wd[c * CW : (c + 1) * CW, :])
    lat_all[me, ep] = latent.astype(BF16)

    def lat_copy(i):
        return pltpu.make_async_remote_copy(
            src_ref=lat_all.at[me, ep],
            dst_ref=lat_all.at[me, ep],
            send_sem=s3.at[i - 1],
            recv_sem=r3.at[i - 1],
            device_id={"ep": ep_peer(i)},
            device_id_type=MESH,
        )

    def w_copy(i):
        return pltpu.make_async_remote_copy(
            src_ref=w_all.at[ep],
            dst_ref=w_all.at[ep],
            send_sem=s3w.at[i - 1],
            recv_sem=r3w.at[i - 1],
            device_id={"ep": ep_peer(i)},
            device_id_type=MESH,
        )

    def fwd_copy(i, k):
        row = ep_peer(E - i)
        return pltpu.make_async_remote_copy(
            src_ref=lat_all.at[me, row],
            dst_ref=lat_all.at[me, row],
            send_sem=s4.at[i, k - 1],
            recv_sem=r4.at[i, k - 1],
            device_id={"tp": tp_peer(k)},
            device_id_type=MESH,
        )

    for i in range(1, E):
        lat_copy(i).start()
    for k in far_first:
        fwd_copy(0, k).start()

    logits = jnp.zeros((R, XA), F32)
    for c in range(NC):
        logits = logits + dot_nt(pieces[c], router[:, c * CW : (c + 1) * CW])
    gates = jax.nn.sigmoid(logits)
    w_all[ep] = kept * gates / jnp.sum(picked * gates, axis=-1, keepdims=True)
    for i in range(1, E):
        w_copy(i).start()

    for i in range(1, E):
        lat_copy(i).wait_recv()
        for k in far_first:
            fwd_copy(i, k).start()
    for i in range(1, E):
        w_copy(i).wait_recv()
    for i in range(E):
        for k in range(1, T):
            fwd_copy(i, k).wait_recv()

    BR = 128 if N % 128 == 0 else R
    NB = N // BR
    per = BR // R
    for load in loads[3:]:
        load.wait()

    for t in range(T):
        lat_mat[:, t * L : (t + 1) * L] = lat_all[t].reshape(N, L)

    def expert(x, carry):
        def rows_step(b, carry):
            rows = pl.ds(pl.multiple_of(b * BR, BR), BR)
            lat = lat_mat[rows, :]
            gate = dot(lat, wg[x])
            upper = dot(lat, wp[x])
            weights = w_all[pl.ds(b * per, per)].reshape(BR, XA)
            lane = lax.broadcasted_iota(jnp.int32, (BR, XA), 1)
            scaled = jnp.sum(
                jnp.where(lane == ep * X + x, weights, 0.0), axis=-1, keepdims=True
            )
            act[x, rows] = (jax.nn.silu(gate) * upper * scaled).astype(BF16)
            return carry

        return lax.fori_loop(0, NB, rows_step, carry)

    lax.fori_loop(0, X, expert, 0)

    def c_copy(k):
        return pltpu.make_async_remote_copy(
            src_ref=c_send.at[k - 1],
            dst_ref=c_recv.at[k - 1],
            send_sem=s5.at[k - 1],
            recv_sem=r5.at[k - 1],
            device_id={"tp": tp_peer(k)},
            device_id_type=MESH,
        )

    def down(k, b):
        rows = pl.ds(pl.multiple_of(b * BR, BR), BR)
        cols = pl.ds(pl.multiple_of(tp_peer(k) * L, L), L)
        value = dot(act[0, rows], wn[0, :, cols])
        for x in range(1, X):
            value = value + dot(act[x, rows], wn[x, :, cols])
        return rows, value

    for k in far_first:

        def send_rows(b, carry):
            rows, value = down(k, b)
            c_send[k - 1, rows] = value.astype(BF16)
            return carry

        lax.fori_loop(0, NB, send_rows, 0)
        c_copy(k).start()

    def own_rows(b, carry):
        rows, value = down(T, b)
        c_own[rows, :] = value
        return carry

    lax.fori_loop(0, NB, own_rows, 0)
    for k in range(1, T):
        c_copy(k).wait_recv()

    def d_copy(i):
        return pltpu.make_async_remote_copy(
            src_ref=d_send.at[ep_peer(i)],
            dst_ref=d_recv.at[i - 1],
            send_sem=s6.at[i - 1],
            recv_sem=r6.at[i - 1],
            device_id={"ep": ep_peer(i)},
            device_id_type=MESH,
        )

    def block_sum(j):
        rows = pl.ds(pl.multiple_of(j * R, R), R)
        value = c_own[rows, :]
        for k in range(1, T):
            value = value + c_recv[k - 1, rows].astype(F32)
        return value

    for i in range(1, E):
        d_send[ep_peer(i)] = block_sum(ep_peer(i)).astype(BF16)
        d_copy(i).start()
    combined = block_sum(ep)
    for i in range(1, E):
        d_copy(i).wait_recv()
        combined = combined + d_recv[i - 1].astype(F32)
    combined = combined.astype(BF16)

    def l_copy(c, k):
        peer = tp_peer(k)
        return pltpu.make_async_remote_copy(
            src_ref=l_send.at[c, peer],
            dst_ref=l_recv.at[c, k - 1],
            send_sem=s7.at[c, k - 1],
            recv_sem=r7.at[c, k - 1],
            device_id={"tp": peer},
            device_id_type=MESH,
        )

    def lift(c, carry):
        cols = pl.ds(pl.multiple_of(c * CW, CW), CW)
        part = dot(combined, wu[:, cols]).reshape(T, r, CW)
        l_own[c] = part
        l_send[c] = part.astype(BF16)
        for k in far_first:
            l_copy(c, k).start()
        return carry

    lax.fori_loop(0, NC, lift, 0)
    for c in range(NC):
        value = res[c] + l_own[c, me]
        for k in range(1, T):
            l_copy(c, k).wait_recv()
            value = value + l_recv[c, k - 1].astype(F32)
        out_ref[:, c * CW : (c + 1) * CW] = value.astype(BF16)

    for k in range(1, T):
        n_copy(k).wait_send()
        c_copy(k).wait_send()
        for c in range(NC):
            p_copy(c, k).wait_send()
            l_copy(c, k).wait_send()
        for i in range(E):
            fwd_copy(i, k).wait_send()
    for i in range(1, E):
        lat_copy(i).wait_send()
        w_copy(i).wait_send()
        d_copy(i).wait_send()


def on_device(
    hidden_in,
    queries,
    new_keys,
    new_values,
    key_cache,
    value_cache,
    lengths,
    out_weight,
    norm_gain,
    router_weight,
    latent_down,
    latent_up,
    gate_weight,
    up_weight,
    down_weight,
    routes,
    slot_index,
):
    T = lax.axis_size("tp")
    E = lax.axis_size("ep")
    R, Hl, HD = queries.shape
    D = hidden_in.shape[1]
    r = R // T
    L = latent_down.shape[1]
    LAT = L * T
    X, _, F = gate_weight.shape
    XA = router_weight.shape[1]
    N, TOPK = routes.shape
    slots_all = 2 * N * TOPK // XA
    NC = 2
    CW = D // NC
    dims = (T, E, R, r, D, NC, L, X, XA, F, N, TOPK, slots_all)
    vmem = pl.BlockSpec(memory_space=pltpu.VMEM)
    smem = pl.BlockSpec(memory_space=pltpu.SMEM)
    hbm = pl.BlockSpec(memory_space=pl.ANY)
    dma = pltpu.SemaphoreType.DMA
    scratch = [
        pltpu.VMEM(key_cache.shape, BF16),
        pltpu.VMEM(value_cache.shape, BF16),
        pltpu.VMEM(out_weight.shape, BF16),
        pltpu.VMEM((XA, D), BF16),
        pltpu.VMEM(latent_down.shape, BF16),
        pltpu.VMEM(latent_up.shape, BF16),
        pltpu.VMEM(gate_weight.shape, BF16),
        pltpu.VMEM(up_weight.shape, BF16),
        pltpu.VMEM(down_weight.shape, BF16),
        pltpu.VMEM((r, D), BF16),
        pltpu.VMEM((R, Hl, HD), F32),
        pltpu.VMEM((NC, T, r, CW), F32),
        pltpu.VMEM((NC, T, r, CW), BF16),
        pltpu.VMEM((NC, T - 1, r, CW), BF16),
        pltpu.VMEM((NC, r, CW), F32),
        pltpu.VMEM((T, NC, r, CW), BF16),
        pltpu.VMEM((T, E, R, L), BF16),
        pltpu.VMEM((N, LAT), BF16),
        pltpu.VMEM((E, R, XA), F32),
        pltpu.VMEM((N, XA), F32),
        pltpu.VMEM((N, XA), F32),
        pltpu.VMEM((X, N, F), BF16),
        pltpu.VMEM((N, L), F32),
        pltpu.VMEM((T - 1, N, L), BF16),
        pltpu.VMEM((T - 1, N, L), BF16),

        pltpu.VMEM((E, R, L), BF16),
        pltpu.VMEM((E - 1, R, L), BF16),
        pltpu.VMEM((NC, T, r, CW), F32),
        pltpu.VMEM((NC, T, r, CW), BF16),
        pltpu.VMEM((NC, T - 1, r, CW), BF16),
        dma((2, R // 8)),
        dma((8,)),
        dma((NC, T - 1)),
        dma((NC, T - 1)),
        dma((T - 1,)),
        dma((T - 1,)),
        dma((E - 1,)),
        dma((E - 1,)),
        dma((E - 1,)),
        dma((E - 1,)),
        dma((E, T - 1)),
        dma((E, T - 1)),
        dma((T - 1,)),
        dma((T - 1,)),
        dma((E - 1,)),
        dma((E - 1,)),
        dma((NC, T - 1)),
        dma((NC, T - 1)),
    ]
    return pl.pallas_call(
        functools.partial(layer_kernel, dims),
        out_shape=jax.ShapeDtypeStruct((r, D), BF16),
        in_specs=[
            hbm,
            vmem,
            vmem,
            vmem,
            hbm,
            hbm,
            smem,
            hbm,
            vmem,
            hbm,
            hbm,
            hbm,
            hbm,
            hbm,
            hbm,
            vmem,
            vmem,
        ],
        out_specs=vmem,
        scratch_shapes=scratch,
        compiler_params=pltpu.CompilerParams(
            collective_id=0, has_side_effects=True, vmem_limit_bytes=60 * 1024 * 1024
        ),
    )(
        hidden_in.reshape(T, r, D),
        queries,
        new_keys,
        new_values,
        key_cache,
        value_cache,
        lengths,
        out_weight,
        norm_gain,
        router_weight.T,
        latent_down,
        latent_up,
        gate_weight,
        up_weight,
        down_weight,
        routes.T,
        slot_index.T,
    )


def solution(mesh):
    return jax.shard_map(
        on_device,
        mesh=mesh,
        in_specs=(
            P(("rep", "ep"), None),
            P(("rep", "ep"), "tp", None),
            P(("rep", "ep"), "tp", None),
            P(("rep", "ep"), "tp", None),
            P(("rep", "ep"), "tp", None, None),
            P(("rep", "ep"), "tp", None, None),
            P(("rep", "ep")),
            P("tp", None),
            P(),
            P(),
            P(None, "tp"),
            P("tp", None),
            P("ep", None, "tp"),
            P("ep", None, "tp"),
            P("ep", "tp", None),
            P("rep", None),
            P("rep", None),
        ),
        out_specs=P(("rep", "ep", "tp"), None),
        check_vma=False,
    )
```
